768 devices in a mesh: mem: 48 (over x, z), ctx: 8 (over y), dp: 2 (over core).
Axes of the slice: x: 4, y: 8, z: 12, core: 2. Of those that a mesh axis runs over, the one named last changes fastest.
Arguments:
- queries: bfloat16 [2, 49152, 32, 128], P('dp', ('mem', 'ctx')), may hold values from -6 to 6
- window_keys: bfloat16 [2, 49152, 32, 128], P('dp', ('mem', 'ctx')), may hold values from -910 to 910
- window_values: bfloat16 [2, 49152, 32, 128], P('dp', ('mem', 'ctx')), may hold values from -6 to 6
- mem_keys: bfloat16 [144, 32, 64, 128], P('mem'), may hold values from -910 to 910
- mem_values: bfloat16 [144, 32, 64, 128], P('mem'), may hold values from -6 to 6
- gate_logit: float32 [32], replicated, may hold values from -3 to 3
- block_ids: int32 [2, 384, 32], P('dp', ('mem', 'ctx')), may hold values from 0 to 143, as said below
Outputs:
- attended: bfloat16 [2, 49152, 32, 128], P('dp', ('mem', 'ctx'))
The draws below stay inside these ranges and needn't reach their ends.
Inputs may be any that keep to these rules, and one draw needn't show every extreme that they name: `block_ids`: block b is held by index b // 3 of mem. Among the 32 blocks of one query block, at most 1 are held by one index of mem, and some index of mem holds exactly 1 of them.
All inputs are finite; a program needn't handle non-finite values.
Results may differ from the reference program's by a relative error of at most 0.013.
Values may be sent and summed in bfloat16 or wider, within the bound.
A program may use at most 64 MiB of HBM per device.

```python
import jax
import jax.numpy as jnp
from jax import lax

H = 32
HD = 128
TOK_DEV = 128
W = 128
BLK = 64
MBLK_DEV = 3
SEQS = 2
NCHUNK = 384
LEN = 49152
MEMBLK = 144


def draw_window_keys(key, part):
    key = jax.random.fold_in(key, 11)
    shape = (SEQS, LEN, H, HD)
    values_out = jnp.clip(jax.random.normal(key, shape, jnp.float32), -6.0, 6.0)
    return values_out.astype(jnp.bfloat16)


def draw_mem_keys(key, part):
    key = jax.random.fold_in(key, 23)
    shape = (MEMBLK, H, BLK, HD)
    values_out = jnp.clip(jax.random.normal(key, shape, jnp.float32), -6.0, 6.0)
    return values_out.astype(jnp.bfloat16)


def draw_block_ids(key, part):
    key = jax.random.fold_in(key, 37)
    owners = MEMBLK // MBLK_DEV
    capacity = (H + owners - 1) // owners
    slot_count = owners * capacity
    row_count = SEQS * NCHUNK
    first, second, third, fourth = jax.random.split(key, 4)
    owner_rank = jax.random.permutation(first, owners)
    hot_owner = (owner_rank < max(1, owners // 4)).astype(jnp.int32)
    slot_owner = jnp.arange(slot_count, dtype=jnp.int32) // capacity
    noise = jax.random.randint(second, (row_count, slot_count), 0, 65536)
    scores = (noise + hot_owner[slot_owner][None, :] * 65536) * slot_count + jnp.arange(slot_count, dtype=jnp.int32)[None, :]
    chosen = lax.top_k(scores, H)[1]
    owner_of = chosen // capacity
    mixing = jax.random.randint(third, (row_count, H), 0, 65536) * H + jnp.arange(H, dtype=jnp.int32)[None, :]
    order = jnp.argsort(mixing, axis=1)
    owner_of = jnp.take_along_axis(owner_of, order, axis=1)
    local_block = jax.random.randint(fourth, (row_count, H), 0, MBLK_DEV)
    return (owner_of * MBLK_DEV + local_block).reshape(SEQS, NCHUNK, H).astype(jnp.int32)


def block_scale(rng, shape, cuts, least, largest):
    gain, own = 1.0, jax.random.fold_in(rng, 6)
    for position, shards_of in cuts:
        draws = jnp.exp(jax.random.uniform(jax.random.fold_in(own, position), (shards_of,), jnp.float32, least / len(cuts), largest / len(cuts)))
        gain = gain * jnp.repeat(draws, shape[position] // shards_of).reshape([-1 if axis == position else 1 for axis in range(len(shape))])
    return gain


def scatter_about(key, dims, deviation, reach, cuts=(), kind=jnp.bfloat16):
    values = deviation * jax.random.normal(key, dims, jnp.float32)
    if cuts:
        values = values * block_scale(key, dims, cuts, -0.22, 0.18)
    return jnp.clip(values, -reach, reach).astype(kind)


def setup_inputs(seed: int = 0) -> dict:
    keys = jax.random.split(jax.random.key(seed), 8)
    return {
        "queries": scatter_about(keys[0], (SEQS, LEN, H, HD), 1.0, 6.0, ((0, 2), (1, 384))),
        "window_keys": draw_window_keys(jax.random.fold_in(keys[7], 71), 0),
        "window_values": scatter_about(keys[2], (SEQS, LEN, H, HD), 1.0, 6.0, ((0, 2), (1, 384))),
        "mem_keys": draw_mem_keys(jax.random.fold_in(keys[7], 71), 0),
        "mem_values": scatter_about(keys[4], (MEMBLK, H, BLK, HD), 1.0, 6.0, ((0, 48),)),
        "gate_logit": jnp.clip(jax.random.uniform(keys[5], (H,), jnp.float32, -3.0, 3.0), -3.0, 3.0),
        "block_ids": draw_block_ids(jax.random.fold_in(keys[7], 71), 0),
    }


def softmax_rows(scores, allowed):
    masked = jnp.where(allowed, scores, -1e30)
    highest = jnp.max(masked, axis=-1, keepdims=True)
    weights = jnp.where(allowed, jnp.exp(masked - highest), 0.0)
    return (weights / jnp.sum(weights, axis=-1, keepdims=True)).astype(jnp.bfloat16)


def local_attention(query_rows, keys_all, values_all, group_start):
    row_count = query_rows.shape[0]
    key_count = keys_all.shape[0]
    reach_back = key_count - row_count
    softmax_scale = HD ** -0.5
    scores = jnp.einsum("qhd,khd->hqk", query_rows.astype(jnp.float32), keys_all.astype(jnp.float32)) * softmax_scale
    query_pos = jnp.arange(row_count, dtype=jnp.int32)[:, None]
    key_pos = jnp.arange(key_count, dtype=jnp.int32)[None, :]
    allowed = (key_pos > query_pos) & (key_pos <= query_pos + reach_back) & (group_start - reach_back + key_pos >= 0)
    weights = softmax_rows(scores, allowed[None])
    return jnp.einsum("hqk,khd->qhd", weights.astype(jnp.float32), values_all.astype(jnp.float32))


def memory_attention(query_rows, picked_keys, picked_values):
    softmax_scale = HD ** -0.5
    scores = jnp.einsum("qhd,hkd->hqk", query_rows.astype(jnp.float32), picked_keys.astype(jnp.float32)) * softmax_scale
    weights = softmax_rows(scores, True)
    result = jnp.einsum("hqk,hkd->qhd", weights.astype(jnp.float32), picked_values.astype(jnp.float32))
    return result.astype(jnp.bfloat16)


def reference(queries, window_keys, window_values, mem_keys, mem_values, gate_logit, block_ids):
    padded_keys = jnp.pad(window_keys, ((0, 0), (W, 0), (0, 0), (0, 0)))
    padded_values = jnp.pad(window_values, ((0, 0), (W, 0), (0, 0), (0, 0)))
    gate_mix = jax.nn.sigmoid(gate_logit.astype(jnp.float32))[None, :, None]
    head_ids = jnp.arange(H, dtype=jnp.int32)

    def one_group(number):
        sequence = (number // NCHUNK).astype(jnp.int32)
        group = (number % NCHUNK).astype(jnp.int32)
        group_start = (group * TOK_DEV).astype(jnp.int32)
        anchor = jnp.zeros((), jnp.int32)
        query_rows = lax.dynamic_slice(queries, (sequence, group_start, anchor, anchor), (1, TOK_DEV, H, HD))[0]
        keys_all = lax.dynamic_slice(padded_keys, (sequence, group_start, anchor, anchor), (1, W + TOK_DEV, H, HD))[0]
        values_all = lax.dynamic_slice(padded_values, (sequence, group_start, anchor, anchor), (1, W + TOK_DEV, H, HD))[0]
        local_out = local_attention(query_rows, keys_all, values_all, group_start)
        wanted = lax.dynamic_slice(block_ids, (sequence, group, anchor), (1, 1, H))[0, 0].astype(jnp.int32)
        picked_keys = mem_keys[wanted, head_ids]
        picked_values = mem_values[wanted, head_ids]
        memory_out = memory_attention(query_rows, picked_keys, picked_values)
        mixed = gate_mix * memory_out.astype(jnp.float32) + (1.0 - gate_mix) * local_out
        return mixed.astype(jnp.bfloat16)

    pieces = lax.map(one_group, jnp.arange(SEQS * NCHUNK, dtype=jnp.int32))
    return pieces.reshape(SEQS, LEN, H, HD)
```

```python
import functools

import jax
import jax.numpy as jnp
from jax import lax
from jax.experimental import pallas as pl
from jax.experimental.pallas import tpu as pltpu
from jax.sharding import PartitionSpec as P

MESH = pl.DeviceIdType.MESH
XN = 4
CHUNK = 32
UNROLL = 4
NEG = -1e30


def dot_nt(a, b):
    return lax.dot_general(a, b, (((1,), (1,)), ((), ())), preferred_element_type=jnp.float32)


def dot_nn(a, b):
    return lax.dot_general(a, b, (((1,), (0,)), ((), ())), preferred_element_type=jnp.float32)


def kernel(
    sizes,
    q_hbm, k_hbm, v_hbm, mk_hbm, mv_hbm, gate_sm, ids_sm, req_hbm,
    out_hbm,
    q_v, k_v, v_v, mk_v, mv_v,
    qn_v, ansn_v, ansp_v, stn_v, stp_v,
    wide, q_t, k_t, v_t, qn_t, own_o, own_m,
    tab_v, tab_sm, blk_send, blk_recv,
    load_sem, q_send, q_recv, a_send, a_recv, s_send, s_recv,
    r_send, r_recv, b_send, b_recv, self_sem, tab_sem, out_sem,
):
    xn, zn, cn, held = sizes
    mem_n = xn * zn
    tok, heads, width = q_v.shape
    blk = mk_v.shape[1]
    scale = width ** (-0.5)
    pieces = tok // CHUNK
    mem, ctx, dp = lax.axis_index("mem"), lax.axis_index("ctx"), lax.axis_index("dp")
    mx, mz = mem // zn, mem % zn
    group = mem * cn + ctx
    total = mem_n * cn
    before = (group + total - 1) % total
    after = (group + 1) % total
    prev = (before // cn, before % cn, dp)
    nxt = (after // cn, after % cn, dp)

    def owner_at(k):
        return ((mx + k // zn) % xn) * zn + (mz + k % zn) % zn

    def asker_at(k):
        return ((mx + xn - k // zn) % xn) * zn + (mz + zn - k % zn) % zn

    loads = [
        pltpu.make_async_copy(src, dst, load_sem.at[i])
        for i, (src, dst) in enumerate(
            ((mk_hbm, mk_v), (mv_hbm, mv_v), (k_hbm, k_v), (v_hbm, v_v), (q_hbm, q_v))
        )
    ]
    for load in loads:
        load.start()
    own_row = pltpu.make_async_copy(req_hbm.at[mem], tab_v.at[0], self_sem)
    own_row.start()

    barrier = pltpu.get_barrier_semaphore()
    pl.semaphore_signal(barrier, inc=1, device_id=prev, device_id_type=MESH)
    pl.semaphore_signal(barrier, inc=1, device_id=nxt, device_id_type=MESH)

    def greet(k, _):
        pl.semaphore_signal(barrier, inc=1, device_id=(owner_at(k), ctx, dp), device_id_type=MESH)
        return 0

    lax.fori_loop(1, mem_n, greet, 0)
    pl.semaphore_wait(barrier, mem_n + 1)

    def ask(k, _):
        owner = owner_at(k)
        pltpu.make_async_remote_copy(
            req_hbm.at[owner], tab_v.at[k], r_send, r_recv, (owner, ctx, dp), MESH
        ).start()
        return 0

    lax.fori_loop(1, mem_n, ask, 0)

    def q_piece(c):
        rows = pl.ds(c * CHUNK, CHUNK)
        return pltpu.make_async_remote_copy(
            q_hbm.at[rows], qn_v.at[rows], q_send.at[c], q_recv.at[c], prev, MESH
        )

    for c in range(pieces):
        q_piece(c).start()

    others = pl.ds(1, mem_n - 1)
    ask_all = pltpu.make_async_remote_copy(
        tab_v.at[others], tab_v.at[others], r_send, r_recv, prev, MESH
    )
    loads[0].wait()
    loads[1].wait()
    own_row.wait()
    ask_all.wait_recv()
    to_scalar = pltpu.make_async_copy(tab_v, tab_sm, tab_sem)
    to_scalar.start()
    to_scalar.wait()

    blk_recv[0, pl.ds(0, blk)] = mk_v[tab_sm[0, 0, 0]]
    blk_recv[0, pl.ds(blk, blk)] = mv_v[tab_sm[0, 0, 0]]

    def serve(k, _):
        which = tab_sm[k, 0, 0]
        blk_send[k, pl.ds(0, blk)] = mk_v[which]
        blk_send[k, pl.ds(blk, blk)] = mv_v[which]
        pltpu.make_async_remote_copy(
            blk_send.at[k], blk_recv.at[k], b_send, b_recv, (asker_at(k), ctx, dp), MESH
        ).start()
        return 0

    lax.fori_loop(1, mem_n, serve, 0)

    def widen(src, first, count):
        step = min(count, 16)

        def one(i, _):
            rows = src[pl.ds(first + i * step, step)].astype(jnp.float32)
            wide[pl.ds(i * step * heads, step * heads)] = rows.reshape(step * heads, width)
            return 0

        lax.fori_loop(0, count // step, one, 0)

    def by_head(dst, first, count):
        def some(i, _):
            for u in range(UNROLL):
                h = i * UNROLL + u
                rows = wide[pl.ds(h, count, stride=heads), :]
                dst[h, pl.ds(first, count), pl.ds(0, width)] = rows.astype(jnp.bfloat16)
            return 0

        lax.fori_loop(0, heads // UNROLL, some, 0)

    for i, (src, dst) in ((2, (k_v, k_t)), (3, (v_v, v_t)), (4, (q_v, q_t))):
        loads[i].wait()
        widen(src, 0, tok)
        by_head(dst, 0, tok)

    def ones_half(h, _):
        v_t[h, :, pl.ds(width, width)] = jnp.ones((tok, width), jnp.bfloat16)
        return 0

    lax.fori_loop(0, heads, ones_half, 0)

    q_pos = lax.broadcasted_iota(jnp.int32, (tok, tok), 0)
    k_pos = lax.broadcasted_iota(jnp.int32, (tok, tok), 1)
    causal = k_pos <= q_pos

    def own(i, _):
        for u in range(UNROLL):
            h = i * UNROLL + u
            scores = jnp.where(causal, dot_nt(q_t[h], k_t[h]) * scale, NEG)
            top = jnp.max(scores, axis=-1, keepdims=True)
            weights = jnp.exp(scores - top).astype(jnp.bfloat16)
            own_o[h] = dot_nn(weights, v_t[h])
            own_m[h] = jnp.broadcast_to(top, (tok, width))
        return 0

    lax.fori_loop(0, heads // UNROLL, own, 0)

    lane = lax.broadcasted_iota(jnp.int32, (CHUNK, width), 1)

    def a_piece(c):
        rows = pl.ds(c * CHUNK, CHUNK)
        return pltpu.make_async_remote_copy(
            ansn_v.at[rows], ansp_v.at[rows], a_send.at[c], a_recv.at[c], nxt, MESH
        )

    def s_piece(c):
        rows = pl.ds(c * CHUNK, CHUNK)
        return pltpu.make_async_remote_copy(
            stn_v.at[rows], stp_v.at[rows], s_send.at[c], s_recv.at[c], nxt, MESH
        )

    for c in range(pieces):
        q_piece(c).wait_recv()
        widen(qn_v, c * CHUNK, CHUNK)
        by_head(qn_t, 0, CHUNK)
        past = k_pos[:CHUNK] > q_pos[:CHUNK] + c * CHUNK

        def partial(i, stats, past=past):
            for u in range(UNROLL):
                h = i * UNROLL + u
                scores = jnp.where(past, dot_nt(qn_t[h], k_t[h]) * scale, NEG)
                top = jnp.max(scores, axis=-1, keepdims=True)
                weights = jnp.where(past, jnp.exp(scores - top), 0.0).astype(jnp.bfloat16)
                summed = dot_nn(weights, v_t[h])
                wide[pl.ds(h, CHUNK, stride=heads), :] = summed[:, :width]
                stats = jnp.where(lane == h, top, stats)
                stats = jnp.where(lane == h + heads, summed[:, width:], stats)
            return stats

        stats = lax.fori_loop(
            0, heads // UNROLL, partial, jnp.zeros((CHUNK, width), jnp.float32)
        )
        stn_v[pl.ds(c * CHUNK, CHUNK)] = stats

        def narrow(i, _, c=c):
            step = 16
            rows = wide[pl.ds(i * step * heads, step * heads)].reshape(step, heads, width)
            ansn_v[pl.ds(c * CHUNK + i * step, step)] = rows.astype(jnp.bfloat16)
            return 0

        lax.fori_loop(0, CHUNK // 16, narrow, 0)
        a_piece(c).start()
        s_piece(c).start()

    lane_all = lax.broadcasted_iota(jnp.int32, (tok, width), 1)
    first_block = group == 0

    for c in range(pieces):
        a_piece(c).wait_recv()
        s_piece(c).wait_recv()
    widen(ansp_v, 0, tok)

    def gate_of(h):
        return 1.0 / (1.0 + jnp.exp(jnp.full((8, width), -gate_sm[h], jnp.float32)))[:1]

    def join(i, _):
        stats = stp_v[...]
        for u in range(UNROLL):
            h = i * UNROLL + u
            top_p = jnp.sum(jnp.where(lane_all == h, stats, 0.0), axis=-1, keepdims=True)
            sum_p = jnp.sum(jnp.where(lane_all == h + heads, stats, 0.0), axis=-1, keepdims=True)
            top_p = jnp.where(first_block, NEG, top_p)
            top_o = own_m[h]
            top = jnp.maximum(top_p, top_o)
            part_p = jnp.exp(top_p - top)
            part_o = jnp.exp(top_o - top)
            mine = own_o[h]
            theirs = wide[pl.ds(h, tok, stride=heads), :]
            above = part_p * theirs + part_o * mine[:, :width]
            below = part_p * sum_p + part_o * mine[:, width:]
            own_m[h] = (1.0 - gate_of(h)) * (above / below)
        return 0

    lax.fori_loop(0, heads // UNROLL, join, 0)

    block_all = pltpu.make_async_remote_copy(
        blk_send.at[others], blk_recv.at[others], b_send, b_recv, prev, MESH
    )
    block_all.wait_recv()

    def recall(i, _):
        for u in range(UNROLL):
            h = i * UNROLL + u
            owner = lax.div(ids_sm[h], held)
            dx = lax.rem(lax.div(owner, zn) - mx + xn, xn)
            dz = lax.rem(lax.rem(owner, zn) - mz + zn, zn)
            block = blk_recv[dx * zn + dz]
            scores = dot_nt(q_t[h], block[:blk]) * scale
            top = jnp.max(scores, axis=-1, keepdims=True)
            weights = jnp.exp(scores - top)
            below = jnp.sum(weights, axis=-1, keepdims=True)
            above = dot_nn(weights.astype(jnp.bfloat16), block[blk:])
            mixed = gate_of(h) * (above / below) + own_m[h]
            wide[pl.ds(h, tok, stride=heads), :] = mixed
        return 0

    lax.fori_loop(0, heads // UNROLL, recall, 0)

    def finish(i, _):
        step = 16
        rows = wide[pl.ds(i * step * heads, step * heads)].reshape(step, heads, width)
        q_v[pl.ds(i * step, step)] = rows.astype(jnp.bfloat16)
        return 0

    lax.fori_loop(0, tok // 16, finish, 0)
    result = pltpu.make_async_copy(q_v, out_hbm, out_sem)
    result.start()
    ask_all.wait_send()
    block_all.wait_send()
    for c in range(pieces):
        q_piece(c).wait_send()
        a_piece(c).wait_send()
        s_piece(c).wait_send()
    result.wait()


def local(queries, window_keys, window_values, mem_keys, mem_values, gate_logit, block_ids):
    _, tok, heads, width = queries.shape
    held, _, blk, _ = mem_keys.shape
    mem_n, cn = lax.axis_size("mem"), lax.axis_size("ctx")
    zn = mem_n // XN
    pieces = tok // CHUNK
    wanted = block_ids[0, 0]
    head_ids = jnp.arange(heads, dtype=jnp.int32)
    entry = (wanted % held) * heads + head_ids
    asked = jnp.where(
        (wanted // held)[None, :] == jnp.arange(mem_n, dtype=jnp.int32)[:, None], entry[None, :], 0
    )
    request = jnp.broadcast_to(jnp.sum(asked, axis=1)[:, None, None], (mem_n, 1, 128))
    anywhere = pl.BlockSpec(memory_space=pl.ANY)
    scalars = pl.BlockSpec(memory_space=pltpu.SMEM)
    bf, f32 = jnp.bfloat16, jnp.float32
    dma = pltpu.SemaphoreType.DMA
    native = pltpu.VMEM((tok, heads, width), bf)
    out = pl.pallas_call(
        functools.partial(kernel, (XN, zn, cn, held)),
        out_shape=jax.ShapeDtypeStruct((tok, heads, width), bf),
        in_specs=[anywhere] * 5 + [scalars, scalars, anywhere],
        out_specs=anywhere,
        scratch_shapes=[
            native, native, native,
            pltpu.VMEM((held * heads, blk, width), bf),
            pltpu.VMEM((held * heads, blk, width), bf),
            native, native, native,
            pltpu.VMEM((tok, width), f32),
            pltpu.VMEM((tok, width), f32),
            pltpu.VMEM((tok * heads, width), f32),
            pltpu.VMEM((heads, tok, width), bf),
            pltpu.VMEM((heads, tok, width), bf),
            pltpu.VMEM((heads, tok, 2 * width), bf),
            pltpu.VMEM((heads, CHUNK, width), bf),
            pltpu.VMEM((heads, tok, 2 * width), f32),
            pltpu.VMEM((heads, tok, width), f32),
            pltpu.VMEM((mem_n, 1, 128), jnp.int32),
            pltpu.SMEM((mem_n, 1, 128), jnp.int32),
            pltpu.VMEM((mem_n, 2 * blk, width), bf),
            pltpu.VMEM((mem_n, 2 * blk, width), bf),
            dma((5,)), dma((pieces,)), dma((pieces,)), dma((pieces,)), dma((pieces,)),
            dma((pieces,)), dma((pieces,)),
            dma, dma, dma, dma, dma, dma, dma,
        ],
        compiler_params=pltpu.CompilerParams(
            collective_id=0, has_side_effects=True, vmem_limit_bytes=56 * 1024 * 1024
        ),
    )(
        queries[0], window_keys[0], window_values[0],
        mem_keys.reshape(held * heads, blk, width), mem_values.reshape(held * heads, blk, width),
        gate_logit, wanted, request,
    )
    return out[None]


def solution(mesh):
    placed = (
        P("dp", ("mem", "ctx"), None, None),
        P("dp", ("mem", "ctx"), None, None),
        P("dp", ("mem", "ctx"), None, None),
        P("mem", None, None, None),
        P("mem", None, None, None),
        P(),
        P("dp", ("mem", "ctx"), None),
    )
    return jax.shard_map(
        local,
        mesh=mesh,
        in_specs=placed,
        out_specs=P("dp", ("mem", "ctx"), None, None),
        check_vma=False,
    )
```

```python
import functools

import jax
import jax.numpy as jnp
from jax import lax
from jax.experimental import pallas as pl
from jax.experimental.pallas import tpu as pltpu
from jax.sharding import PartitionSpec as P

MESH = pl.DeviceIdType.MESH
XN = 4
CHUNK = 32
UNROLL = 4
NEG = -1e30
AHEAD = 4
DOWN, UP = 17, 28
BOTH, NOT_FIRST, NOT_LAST = range(3)
PLAN = (
    ((20, 4, NOT_FIRST), (28, 4, NOT_LAST)),
    ((17, 3, NOT_FIRST), (32, 3, NOT_LAST), (16, 1, BOTH), (35, 1, BOTH)),
    ((12, 4, BOTH), (36, 4, BOTH)),
    ((8, 4, BOTH), (40, 4, BOTH)),
    ((24, 3, BOTH), (1, 3, BOTH), (27, 1, BOTH)),
    ((4, 4, BOTH), (44, 4, BOTH)),
)
EXTRA = 1


def dot_nt(a, b):
    return lax.dot_general(a, b, (((1,), (1,)), ((), ())), preferred_element_type=jnp.float32)


def dot_nn(a, b):
    return lax.dot_general(a, b, (((1,), (0,)), ((), ())), preferred_element_type=jnp.float32)


def kernel(
    sizes,
    q_hbm, k_hbm, v_hbm, mk_hbm, mv_hbm, gate_sm, ids_sm, req_hbm,
    out_hbm,
    q_v, k_v, v_v, mk_v, mv_v,
    qn_v, ansn_v, ansp_v, stn_v, stp_v,
    q_t, k_t, v_t, qn_t, an_t, ap_t, own_o, own_m, mem_w,
    tab_v, tab_sm, mk_send, mk_recv, mv_send, mv_recv,
    load_sem, q_send, q_recv, a_send, a_recv, s_send, s_recv, far_send, far_recv,
    r_send, r_recv, b_send, b_recv, self_sem, tab_sem, out_sem,
):
    xn, zn, cn, held = sizes
    mem_n = xn * zn
    tok, heads, width = q_v.shape
    blk = mk_v.shape[1]
    scale = width ** (-0.5)
    sub = tok // cn
    mem, ctx, dp = lax.axis_index("mem"), lax.axis_index("ctx"), lax.axis_index("dp")
    mx, mz = mem // zn, mem % zn
    group = mem * cn + ctx
    total = mem_n * cn
    before = (group + total - 1) % total
    after = (group + 1) % total
    prev = (before // cn, before % cn, dp)
    nxt = (after // cn, after % cn, dp)
    first_ctx, last_ctx = ctx == 0, ctx == cn - 1
    not_first, not_last = ctx > 0, ctx < cn - 1
    down, up = DOWN + ctx - 1, UP + ctx

    def owner_at(k):
        return ((mx + k % xn) % xn) * zn + (mz + k // xn) % zn

    def asker_at(k):
        return ((mx + xn - k % xn) % xn) * zn + (mz + zn - k // xn) % zn

    loads = [
        pltpu.make_async_copy(src, dst, load_sem.at[i])
        for i, (src, dst) in enumerate(
            ((k_hbm, k_v), (mk_hbm, mk_v), (mv_hbm, mv_v), (v_hbm, v_v), (q_hbm, q_v))
        )
    ]
    for load in loads:
        load.start()
    own_row = pltpu.make_async_copy(req_hbm.at[mem], tab_v.at[0], self_sem)
    own_row.start()

    barrier = pltpu.get_barrier_semaphore()

    def greet(k, _):
        pl.semaphore_signal(barrier, inc=1, device_id=(owner_at(k), ctx, dp), device_id_type=MESH)
        return 0

    lax.fori_loop(1, mem_n, greet, 0)

    def greet_at(there):
        pl.semaphore_signal(barrier, inc=1, device_id=there, device_id_type=MESH)

    greet_at(prev)
    greet_at(nxt)

    @pl.when(first_ctx)
    def _():
        for j in range(1, cn):
            greet_at((owner_at(DOWN + j - 1), j, dp))

    @pl.when(last_ctx)
    def _():
        for j in range(cn - 1):
            greet_at((owner_at(UP + j), j, dp))

    pl.when(not_first)(lambda: greet_at((asker_at(down), 0, dp)))
    pl.when(not_last)(lambda: greet_at((asker_at(up), cn - 1, dp)))
    pl.when(first_ctx | last_ctx)(lambda: pl.semaphore_wait(barrier, mem_n + 1 + cn))
    pl.when(not_first & not_last)(lambda: pl.semaphore_wait(barrier, mem_n + 1 + 2))

    def ask(k, _):
        owner = owner_at(k)
        pltpu.make_async_remote_copy(
            req_hbm.at[owner], tab_v.at[k], r_send, r_recv, (owner, ctx, dp), MESH
        ).start()
        return 0

    lax.fori_loop(1, mem_n, ask, 0)

    def ask_aside(k, j, i):
        owner = owner_at(k)
        return pltpu.make_async_remote_copy(
            req_hbm.at[owner], tab_v.at[mem_n + i], far_send.at[j], far_recv.at[i], (owner, j, dp), MESH
        )

    @pl.when(first_ctx)
    def _():
        for j in range(1, cn):
            ask_aside(DOWN + j - 1, j, 0).start()

    @pl.when(last_ctx)
    def _():
        for j in range(cn - 1):
            ask_aside(UP + j, j, 1).start()

    def rows_of(c):
        return pl.ds(c * sub, sub)

    def q_direct(c):
        return pltpu.make_async_remote_copy(
            q_hbm.at[rows_of(c)], qn_v.at[rows_of(c)], q_send.at[c], q_recv.at[c], prev, MESH
        )

    def q_start(c):
        q_direct(c).start()

    for c in range(min(4, cn)):
        q_start(c)

    def by_head(dst, src, first, count):
        def one(i, _):
            rows = src[pl.ds(first + i * 16, 16)]
            dst[:, pl.ds(i * 16, 16), pl.ds(0, width)] = jnp.swapaxes(rows, 0, 1)
            return 0

        lax.fori_loop(0, count // 16, one, 0)

    def by_position(dst, src, first, count):
        def one(i, _):
            dst[pl.ds(first + i * 16, 16)] = jnp.swapaxes(src[:, pl.ds(i * 16, 16), :], 0, 1)
            return 0

        lax.fori_loop(0, count // 16, one, 0)

    def some_heads(count, body, init=0, first=0, last=heads):
        def one(i, carry):
            return body([i * count + u for u in range(count)], carry)

        return lax.fori_loop(first // count, last // count, one, init)

    loads[0].wait()
    by_head(k_t, k_v, 0, tok)

    others = pl.ds(1, mem_n - 1)
    ask_all = pltpu.make_async_remote_copy(
        tab_v.at[others], tab_v.at[others], r_send, r_recv, prev, MESH
    )
    loads[1].wait()
    own_row.wait()
    ask_all.wait_recv()
    pl.when(not_first)(lambda: ask_aside(0, 0, 0).wait_recv())
    pl.when(not_last)(lambda: ask_aside(0, 0, 1).wait_recv())
    to_scalar = pltpu.make_async_copy(tab_v, tab_sm, tab_sem)
    to_scalar.start()
    to_scalar.wait()

    batches = len(PLAN)
    who = {BOTH: None, NOT_FIRST: not_first, NOT_LAST: not_last}
    extras = {(EXTRA, NOT_FIRST): (mem_n, down, 0), (EXTRA, NOT_LAST): (mem_n + 1, up, cn - 1)}

    def guarded(part, act):
        if who[part] is None:
            act()
        else:
            pl.when(who[part])(act)

    def batch_done(i):
        send = (mk_send, mv_send)[i // batches]
        for r, (first, count, part) in enumerate(PLAN[i % batches]):
            sent = pl.ds(0, count + int((i % batches, part) in extras))
            copy = pltpu.make_async_remote_copy(
                send.at[sent], send.at[sent], b_send.at[i, r], b_recv.at[0], prev, MESH
            )
            guarded(part, copy.wait_send)

    def serve(i):
        send, recv = ((mk_send, mk_recv), (mv_send, mv_recv))[i // batches]
        held_v = (mk_v, mv_v)[i // batches]
        if i >= AHEAD:
            batch_done(i - AHEAD)
        if i % batches == 0:
            recv[0] = held_v[tab_sm[0, 0, 0]]

        def push(k, to, r, there):
            send[k] = held_v[tab_sm[k, 0, 0]]
            pltpu.make_async_remote_copy(
                send.at[k], recv.at[to], b_send.at[i, r], b_recv.at[i // batches], there, MESH
            ).start()

        ranges = PLAN[i % batches]
        for r, (first, count, part) in enumerate(ranges):
            if (i % batches, part) in extras:
                k, to, there = extras[i % batches, part]
                guarded(part, lambda k=k, to=to, r=r, y=there: push(k, to, r, (asker_at(to), y, dp)))

        def some(t, _):
            for r, (first, count, part) in enumerate(ranges):
                if count > 1:
                    k = first + t
                    guarded(part, lambda k=k, r=r: push(k, k, r, (asker_at(k), ctx, dp)))
            return 0

        lax.fori_loop(0, min([count for _, count, _ in ranges if count > 1] or [0]), some, 0)
        for r, (first, count, part) in enumerate(ranges):
            if count == 1:
                guarded(part, lambda k=first, r=r: push(k, k, r, (asker_at(k), ctx, dp)))

    steps = iter(range(2 * batches))

    def pump():
        for i in steps:
            serve(i)
            return

    loads[2].wait()
    pump()
    pump()
    for c in range(4, cn):
        q_start(c)
    pump()

    for i, (src, dst) in ((3, (v_v, v_t)), (4, (q_v, q_t))):
        loads[i].wait()
        by_head(dst, src, 0, tok)
    pump()

    def ones_half(h, _):
        v_t[h, :, pl.ds(width, width)] = jnp.ones((tok, width), jnp.bfloat16)
        return 0

    lax.fori_loop(0, heads, ones_half, 0)

    q_pos = lax.broadcasted_iota(jnp.int32, (tok, tok), 0)
    k_pos = lax.broadcasted_iota(jnp.int32, (tok, tok), 1)

    lane = lax.broadcasted_iota(jnp.int32, (CHUNK, width), 1)

    def a_direct(c):
        return pltpu.make_async_remote_copy(
            ansn_v.at[rows_of(c)], ansp_v.at[rows_of(c)], a_send.at[c], a_recv.at[c], nxt, MESH
        )

    def s_piece(c):
        rows = pl.ds(c * CHUNK, CHUNK)
        return pltpu.make_async_remote_copy(
            stn_v.at[rows], stp_v.at[rows], s_send.at[c], s_recv.at[c], nxt, MESH
        )

    per = CHUNK // sub

    def answer(c):
        for j in range(c * per, (c + 1) * per):
            q_direct(j).wait_recv()
        by_head(qn_t, qn_v, c * CHUNK, CHUNK)
        past = k_pos[:CHUNK] > q_pos[:CHUNK] + c * CHUNK

        def partial(hs, stats):
            scores = [dot_nt(qn_t[h], k_t[h]) for h in hs]
            scores = [jnp.where(past, x * scale, NEG) for x in scores]
            tops = [jnp.max(x, axis=-1, keepdims=True) for x in scores]
            weights = [jnp.where(past, jnp.exp(x - t), 0.0) for x, t in zip(scores, tops)]
            summed = [dot_nn(w.astype(jnp.bfloat16), v_t[h]) for w, h in zip(weights, hs)]
            for h, x, t in zip(hs, summed, tops):
                an_t[h] = x[:, :width].astype(jnp.bfloat16)
                stats = jnp.where(lane == h, t, stats)
                stats = jnp.where(lane == h + heads, x[:, width:], stats)
            return stats

        stn_v[pl.ds(c * CHUNK, CHUNK)] = some_heads(
            min(8, heads), partial, jnp.zeros((CHUNK, width), jnp.float32)
        )
        by_position(ansn_v, an_t, c * CHUNK, CHUNK)
        for j in range(c * per, (c + 1) * per):
            a_direct(j).start()
        s_piece(c).start()

    causal = k_pos <= q_pos

    def own(hs, _):
        scores = [dot_nt(q_t[h], k_t[h]) for h in hs]
        scores = [jnp.where(causal, x * scale, NEG) for x in scores]
        tops = [jnp.max(x, axis=-1, keepdims=True) for x in scores]
        weights = [jnp.exp(x - t).astype(jnp.bfloat16) for x, t in zip(scores, tops)]
        summed = [dot_nn(w, v_t[h]) for w, h in zip(weights, hs)]
        for h, x, t in zip(hs, summed, tops):
            own_o[h] = x
            own_m[h] = jnp.broadcast_to(t, (tok, width))
        return 0

    pieces = tok // CHUNK
    for c in range(pieces // 2):
        answer(c)
        pump()
    some_heads(UNROLL, own)
    pump()
    for c in range(pieces // 2, pieces):
        answer(c)
        pump()
    for _ in range(2 * batches):
        pump()

    def gate_of(h):
        return 1.0 / (1.0 + jnp.exp(jnp.full((8, width), -gate_sm[h], jnp.float32)))[:1]

    def slot_of(h):
        owner = lax.div(ids_sm[h], held)
        dx = lax.rem(lax.div(owner, zn) - mx + xn, xn)
        dz = lax.rem(lax.rem(owner, zn) - mz + zn, zn)
        return dz * xn + dx

    def fetched(send, recv, i):
        return pltpu.make_async_remote_copy(
            send.at[others], recv.at[others], b_send.at[0], b_recv.at[i], prev, MESH
        )

    fetched(mk_send, mk_recv, 0).wait_recv()

    def weigh(hs, _):
        scores = [dot_nt(q_t[h], mk_recv[slot_of(h)]) * scale for h in hs]
        tops = [jnp.max(x, axis=-1, keepdims=True) for x in scores]
        weights = [jnp.exp(x - t) for x, t in zip(scores, tops)]
        sums = [jnp.sum(w, axis=-1, keepdims=True) for w in weights]
        for h, w, below in zip(hs, weights, sums):
            mem_w[h] = (w * (gate_of(h)[:, :blk] / below)).astype(jnp.bfloat16)
        return 0

    some_heads(UNROLL, weigh)

    lane_all = lax.broadcasted_iota(jnp.int32, (tok, width), 1)
    first_block = group == 0
    for c in range(cn):
        a_direct(c).wait_recv()
    for c in range(pieces):
        s_piece(c).wait_recv()
    by_head(ap_t, ansp_v, 0, tok)

    def join(hs, _):
        stats = stp_v[...]
        tops_p = [jnp.where(lane_all == h, stats, 0.0) for h in hs]
        sums_p = [jnp.where(lane_all == h + heads, stats, 0.0) for h in hs]
        tops_p = [jnp.sum(x, axis=-1, keepdims=True) for x in tops_p]
        sums_p = [jnp.sum(x, axis=-1, keepdims=True) for x in sums_p]
        for h, top_p, sum_p in zip(hs, tops_p, sums_p):
            top_p = jnp.where(first_block, NEG, top_p)
            top_o = own_m[h]
            top = jnp.maximum(top_p, top_o)
            part_p = jnp.exp(top_p - top)
            part_o = jnp.exp(top_o - top)
            mine = own_o[h]
            above = part_p * ap_t[h].astype(jnp.float32) + part_o * mine[:, :width]
            below = part_p * sum_p + part_o * mine[:, width:]
            own_m[h] = (1.0 - gate_of(h)) * (above / below)
        return 0

    some_heads(UNROLL, join)

    fetched(mv_send, mv_recv, 1).wait_recv()

    def recall(hs, _):
        found = [dot_nn(mem_w[h], mv_recv[slot_of(h)]) for h in hs]
        for h, x in zip(hs, found):
            ap_t[h] = (x + own_m[h]).astype(jnp.bfloat16)
        return 0

    some_heads(min(8, heads), recall)
    by_position(q_v, ap_t, 0, tok)
    result = pltpu.make_async_copy(q_v, out_hbm, out_sem)
    result.start()
    ask_all.wait_send()
    for i in range(max(0, 2 * batches - AHEAD), 2 * batches):
        batch_done(i)
    for c in range(cn):
        q_direct(c).wait_send()
        a_direct(c).wait_send()
    for c in range(pieces):
        s_piece(c).wait_send()

    @pl.when(first_ctx)
    def _():
        for j in range(1, cn):
            ask_aside(DOWN + j - 1, j, 0).wait_send()

    @pl.when(last_ctx)
    def _():
        for j in range(cn - 1):
            ask_aside(UP + j, j, 1).wait_send()

    result.wait()


def local(queries, window_keys, window_values, mem_keys, mem_values, gate_logit, block_ids):
    _, tok, heads, width = queries.shape
    held, _, blk, _ = mem_keys.shape
    mem_n, cn = lax.axis_size("mem"), lax.axis_size("ctx")
    zn = mem_n // XN
    pieces = tok // CHUNK
    wanted = block_ids[0, 0]
    head_ids = jnp.arange(heads, dtype=jnp.int32)
    entry = (wanted % held) * heads + head_ids
    asked = jnp.where(
        (wanted // held)[None, :] == jnp.arange(mem_n, dtype=jnp.int32)[:, None], entry[None, :], 0
    )
    request = jnp.broadcast_to(jnp.sum(asked, axis=1)[:, None, None], (mem_n, 1, 128))
    anywhere = pl.BlockSpec(memory_space=pl.ANY)
    scalars = pl.BlockSpec(memory_space=pltpu.SMEM)
    bf, f32 = jnp.bfloat16, jnp.float32
    dma = pltpu.SemaphoreType.DMA
    native = pltpu.VMEM((tok, heads, width), bf)
    slots = pltpu.VMEM((mem_n + 2, blk, width), bf)
    out = pl.pallas_call(
        functools.partial(kernel, (XN, zn, cn, held)),
        out_shape=jax.ShapeDtypeStruct((tok, heads, width), bf),
        in_specs=[anywhere] * 5 + [scalars, scalars, anywhere],
        out_specs=anywhere,
        scratch_shapes=[
            native, native, native,
            pltpu.VMEM((held * heads, blk, width), bf),
            pltpu.VMEM((held * heads, blk, width), bf),
            native, native, native,
            pltpu.VMEM((tok, width), f32),
            pltpu.VMEM((tok, width), f32),
            pltpu.VMEM((heads, tok, width), bf),
            pltpu.VMEM((heads, tok, width), bf),
            pltpu.VMEM((heads, tok, 2 * width), bf),
            pltpu.VMEM((heads, CHUNK, width), bf),
            pltpu.VMEM((heads, CHUNK, width), bf),
            pltpu.VMEM((heads, tok, width), bf),
            pltpu.VMEM((heads, tok, 2 * width), f32),
            pltpu.VMEM((heads, tok, width), f32),
            pltpu.VMEM((heads, tok, blk), bf),
            pltpu.VMEM((mem_n + 2, 1, 128), jnp.int32),
            pltpu.SMEM((mem_n + 2, 1, 128), jnp.int32),
            slots, slots, slots, slots,
            dma((5,)), dma((cn,)), dma((cn,)), dma((cn,)), dma((cn,)),
            dma((pieces,)), dma((pieces,)), dma((cn,)), dma((2,)),
            dma, dma, dma((2 * len(PLAN), 4)), dma((2,)), dma, dma, dma,
        ],
        compiler_params=pltpu.CompilerParams(
            collective_id=0, has_side_effects=True, vmem_limit_bytes=56 * 1024 * 1024
        ),
    )(
        queries[0], window_keys[0], window_values[0],
        mem_keys.reshape(held * heads, blk, width), mem_values.reshape(held * heads, blk, width),
        gate_logit, wanted, request,
    )
    return out[None]


def solution(mesh):
    placed = (
        P("dp", ("mem", "ctx"), None, None),
        P("dp", ("mem", "ctx"), None, None),
        P("dp", ("mem", "ctx"), None, None),
        P("mem", None, None, None),
        P("mem", None, None, None),
        P(),
        P("dp", ("mem", "ctx"), None),
    )
    return jax.shard_map(
        local,
        mesh=mesh,
        in_specs=placed,
        out_specs=P("dp", ("mem", "ctx"), None, None),
        check_vma=False,
    )
```

```python
import functools

import jax
import jax.numpy as jnp
from jax import lax
from jax.experimental import pallas as pl
from jax.experimental.pallas import tpu as pltpu
from jax.sharding import PartitionSpec as P

MESH = pl.DeviceIdType.MESH
XN = 4
CHUNK = 32
UNROLL = 4
NEG = -1e30
AHEAD = 4
DOWN, UP = 17, 28
BOTH, NOT_FIRST, NOT_LAST = range(3)
PLAN = (
    ((20, 4, NOT_FIRST), (28, 4, NOT_LAST)),
    ((17, 3, NOT_FIRST), (32, 3, NOT_LAST), (16, 1, BOTH), (35, 1, BOTH)),
    ((12, 4, BOTH), (36, 4, BOTH)),
    ((8, 4, BOTH), (40, 4, BOTH)),
    ((24, 3, BOTH), (1, 3, BOTH), (27, 1, BOTH)),
    ((4, 4, BOTH), (44, 4, BOTH)),
)
EXTRA = 1


def dot_nt(a, b):
    return lax.dot_general(a, b, (((1,), (1,)), ((), ())), preferred_element_type=jnp.float32)


def dot_nn(a, b):
    return lax.dot_general(a, b, (((1,), (0,)), ((), ())), preferred_element_type=jnp.float32)


def kernel(
    sizes,
    q_hbm, k_hbm, v_hbm, mk_hbm, mv_hbm, gate_sm, ids_sm, ids_hbm,
    out_hbm,
    q_v, k_v, v_v, mk_v, mv_v,
    qn_v, ansn_v, ansp_v, stn_v, stp_v,
    q_t, k_t, v_t, qn_t, an_t, ap_t, own_o, own_m, mem_w,
    tab_v, entry_v, tab_sm, mk_send, mk_recv, mv_send, mv_recv,
    load_sem, q_send, q_recv, a_send, a_recv, s_send, s_recv, far_send, far_recv,
    r_send, r_recv, b_send, b_recv, self_sem, tab_sem, out_sem,
):
    xn, zn, cn, held = sizes
    mem_n = xn * zn
    tok, heads, width = q_v.shape
    blk = mk_v.shape[1]
    scale = width ** (-0.5)
    sub = tok // cn
    mem, ctx, dp = lax.axis_index("mem"), lax.axis_index("ctx"), lax.axis_index("dp")
    mx, mz = mem // zn, mem % zn
    group = mem * cn + ctx
    total = mem_n * cn
    before = (group + total - 1) % total
    after = (group + 1) % total
    prev = (before // cn, before % cn, dp)
    nxt = (after // cn, after % cn, dp)
    first_ctx, last_ctx = ctx == 0, ctx == cn - 1
    not_first, not_last = ctx > 0, ctx < cn - 1
    down, up = DOWN + ctx - 1, UP + ctx

    def owner_at(k):
        return ((mx + k % xn) % xn) * zn + (mz + k // xn) % zn

    def asker_at(k):
        return ((mx + xn - k % xn) % xn) * zn + (mz + zn - k // xn) % zn

    loads = [
        pltpu.make_async_copy(src, dst, load_sem.at[i])
        for i, (src, dst) in enumerate(
            ((k_hbm, k_v), (mk_hbm, mk_v), (mv_hbm, mv_v), (v_hbm, v_v), (q_hbm, q_v))
        )
    ]
    for load in loads:
        load.start()
    own_row = pltpu.make_async_copy(ids_hbm, tab_v.at[0], self_sem)
    own_row.start()

    barrier = pltpu.get_barrier_semaphore()

    def greet(k, _):
        pl.semaphore_signal(barrier, inc=1, device_id=(owner_at(k), ctx, dp), device_id_type=MESH)
        return 0

    lax.fori_loop(1, mem_n, greet, 0)

    def greet_at(there):
        pl.semaphore_signal(barrier, inc=1, device_id=there, device_id_type=MESH)

    greet_at(prev)
    greet_at(nxt)

    @pl.when(first_ctx)
    def _():
        for j in range(1, cn):
            greet_at((owner_at(DOWN + j - 1), j, dp))

    @pl.when(last_ctx)
    def _():
        for j in range(cn - 1):
            greet_at((owner_at(UP + j), j, dp))

    pl.when(not_first)(lambda: greet_at((asker_at(down), 0, dp)))
    pl.when(not_last)(lambda: greet_at((asker_at(up), cn - 1, dp)))
    pl.when(first_ctx | last_ctx)(lambda: pl.semaphore_wait(barrier, mem_n + 1 + cn))
    pl.when(not_first & not_last)(lambda: pl.semaphore_wait(barrier, mem_n + 1 + 2))

    def ask(k, _):
        owner = owner_at(k)
        pltpu.make_async_remote_copy(
            ids_hbm, tab_v.at[k], r_send, r_recv, (owner, ctx, dp), MESH
        ).start()
        return 0

    lax.fori_loop(1, mem_n, ask, 0)

    def ask_aside(k, j, i):
        owner = owner_at(k)
        return pltpu.make_async_remote_copy(
            ids_hbm, tab_v.at[mem_n + i], far_send.at[j], far_recv.at[i], (owner, j, dp), MESH
        )

    @pl.when(first_ctx)
    def _():
        for j in range(1, cn):
            ask_aside(DOWN + j - 1, j, 0).start()

    @pl.when(last_ctx)
    def _():
        for j in range(cn - 1):
            ask_aside(UP + j, j, 1).start()

    def rows_of(c):
        return pl.ds(c * sub, sub)

    def q_direct(c):
        return pltpu.make_async_remote_copy(
            q_hbm.at[rows_of(c)], qn_v.at[rows_of(c)], q_send.at[c], q_recv.at[c], prev, MESH
        )

    def q_start(c):
        q_direct(c).start()

    for c in range(min(4, cn)):
        q_start(c)

    def by_head(dst, src, first, count):
        def one(i, _):
            rows = src[pl.ds(first + i * 16, 16)]
            dst[:, pl.ds(i * 16, 16), pl.ds(0, width)] = jnp.swapaxes(rows, 0, 1)
            return 0

        lax.fori_loop(0, count // 16, one, 0)

    def by_position(dst, src, first, count):
        def one(i, _):
            dst[pl.ds(first + i * 16, 16)] = jnp.swapaxes(src[:, pl.ds(i * 16, 16), :], 0, 1)
            return 0

        lax.fori_loop(0, count // 16, one, 0)

    def some_heads(count, body, init=0, first=0, last=heads):
        def one(i, carry):
            return body([i * count + u for u in range(count)], carry)

        return lax.fori_loop(first // count, last // count, one, init)

    loads[0].wait()
    by_head(k_t, k_v, 0, tok)

    others = pl.ds(1, mem_n - 1)
    ask_all = pltpu.make_async_remote_copy(
        tab_v.at[others], tab_v.at[others], r_send, r_recv, prev, MESH
    )
    loads[1].wait()
    own_row.wait()
    ask_all.wait_recv()
    pl.when(not_first)(lambda: ask_aside(0, 0, 0).wait_recv())
    pl.when(not_last)(lambda: ask_aside(0, 0, 1).wait_recv())
    inside = tab_v[:, 0, :] - mem * held
    head_of = lax.broadcasted_iota(jnp.int32, inside.shape, 1)
    entry = jnp.where((inside >= 0) & (inside < held), inside * heads + head_of, 0)
    entry = jnp.sum(entry, axis=-1, keepdims=True)
    entry = jnp.clip(entry, 0, held * heads - 1)
    entry_v[...] = jnp.broadcast_to(entry, entry_v.shape)
    to_scalar = pltpu.make_async_copy(entry_v, tab_sm, tab_sem)
    to_scalar.start()
    to_scalar.wait()

    batches = len(PLAN)
    who = {BOTH: None, NOT_FIRST: not_first, NOT_LAST: not_last}
    extras = {(EXTRA, NOT_FIRST): (mem_n, down, 0), (EXTRA, NOT_LAST): (mem_n + 1, up, cn - 1)}

    def guarded(part, act):
        if who[part] is None:
            act()
        else:
            pl.when(who[part])(act)

    def batch_done(i):
        send = (mk_send, mv_send)[i // batches]
        for r, (first, count, part) in enumerate(PLAN[i % batches]):
            sent = pl.ds(0, count + int((i % batches, part) in extras))
            copy = pltpu.make_async_remote_copy(
                send.at[sent], send.at[sent], b_send.at[i, r], b_recv.at[0], prev, MESH
            )
            guarded(part, copy.wait_send)

    def serve(i):
        send, recv = ((mk_send, mk_recv), (mv_send, mv_recv))[i // batches]
        held_v = (mk_v, mv_v)[i // batches]
        if i >= AHEAD:
            batch_done(i - AHEAD)
        if i % batches == 0:
            recv[0] = held_v[tab_sm[0, 0]]

        def push(k, to, r, there):
            send[k] = held_v[tab_sm[k, 0]]
            pltpu.make_async_remote_copy(
                send.at[k], recv.at[to], b_send.at[i, r], b_recv.at[i // batches], there, MESH
            ).start()

        ranges = PLAN[i % batches]
        for r, (first, count, part) in enumerate(ranges):
            if (i % batches, part) in extras:
                k, to, there = extras[i % batches, part]
                guarded(part, lambda k=k, to=to, r=r, y=there: push(k, to, r, (asker_at(to), y, dp)))

        def some(t, _):
            for r, (first, count, part) in enumerate(ranges):
                if count > 1:
                    k = first + t
                    guarded(part, lambda k=k, r=r: push(k, k, r, (asker_at(k), ctx, dp)))
            return 0

        lax.fori_loop(0, min([count for _, count, _ in ranges if count > 1] or [0]), some, 0)
        for r, (first, count, part) in enumerate(ranges):
            if count == 1:
                guarded(part, lambda k=first, r=r: push(k, k, r, (asker_at(k), ctx, dp)))

    steps = iter(range(2 * batches))

    def pump():
        for i in steps:
            serve(i)
            return

    loads[2].wait()
    pump()
    pump()
    for c in range(4, cn):
        q_start(c)
    pump()

    for i, (src, dst) in ((3, (v_v, v_t)), (4, (q_v, q_t))):
        loads[i].wait()
        by_head(dst, src, 0, tok)
    pump()

    def ones_half(h, _):
        v_t[h, :, pl.ds(width, width)] = jnp.ones((tok, width), jnp.bfloat16)
        return 0

    lax.fori_loop(0, heads, ones_half, 0)

    q_pos = lax.broadcasted_iota(jnp.int32, (tok, tok), 0)
    k_pos = lax.broadcasted_iota(jnp.int32, (tok, tok), 1)

    lane = lax.broadcasted_iota(jnp.int32, (CHUNK, width), 1)

    def a_direct(c):
        return pltpu.make_async_remote_copy(
            ansn_v.at[rows_of(c)], ansp_v.at[rows_of(c)], a_send.at[c], a_recv.at[c], nxt, MESH
        )

    def s_piece(c):
        rows = pl.ds(c * CHUNK, CHUNK)
        return pltpu.make_async_remote_copy(
            stn_v.at[rows], stp_v.at[rows], s_send.at[c], s_recv.at[c], nxt, MESH
        )

    per = CHUNK // sub

    def answer(c):
        for j in range(c * per, (c + 1) * per):
            q_direct(j).wait_recv()
        by_head(qn_t, qn_v, c * CHUNK, CHUNK)
        past = k_pos[:CHUNK] > q_pos[:CHUNK] + c * CHUNK

        def partial(hs, stats):
            scores = [dot_nt(qn_t[h], k_t[h]) for h in hs]
            scores = [jnp.where(past, x * scale, NEG) for x in scores]
            tops = [jnp.max(x, axis=-1, keepdims=True) for x in scores]
            weights = [jnp.where(past, jnp.exp(x - t), 0.0) for x, t in zip(scores, tops)]
            summed = [dot_nn(w.astype(jnp.bfloat16), v_t[h]) for w, h in zip(weights, hs)]
            for h, x, t in zip(hs, summed, tops):
                an_t[h] = x[:, :width].astype(jnp.bfloat16)
                stats = jnp.where(lane == h, t, stats)
                stats = jnp.where(lane == h + heads, x[:, width:], stats)
            return stats

        stn_v[pl.ds(c * CHUNK, CHUNK)] = some_heads(
            min(8, heads), partial, jnp.zeros((CHUNK, width), jnp.float32)
        )
        by_position(ansn_v, an_t, c * CHUNK, CHUNK)
        for j in range(c * per, (c + 1) * per):
            a_direct(j).start()
        s_piece(c).start()

    causal = k_pos <= q_pos

    def own(hs, _):
        scores = [dot_nt(q_t[h], k_t[h]) for h in hs]
        scores = [jnp.where(causal, x * scale, NEG) for x in scores]
        tops = [jnp.max(x, axis=-1, keepdims=True) for x in scores]
        weights = [jnp.exp(x - t).astype(jnp.bfloat16) for x, t in zip(scores, tops)]
        summed = [dot_nn(w, v_t[h]) for w, h in zip(weights, hs)]
        for h, x, t in zip(hs, summed, tops):
            own_o[h] = x
            own_m[h] = jnp.broadcast_to(t, (tok, width))
        return 0

    pieces = tok // CHUNK
    for c in range(pieces // 2):
        answer(c)
        pump()
    some_heads(UNROLL, own)
    pump()
    for c in range(pieces // 2, pieces):
        answer(c)
        pump()
    for _ in range(2 * batches):
        pump()

    def gate_of(h):
        return 1.0 / (1.0 + jnp.exp(jnp.full((8, width), -gate_sm[h], jnp.float32)))[:1]

    def slot_of(h):
        owner = lax.div(ids_sm[h], held)
        dx = lax.rem(lax.div(owner, zn) - mx + xn, xn)
        dz = lax.rem(lax.rem(owner, zn) - mz + zn, zn)
        return dz * xn + dx

    def fetched(send, recv, i):
        return pltpu.make_async_remote_copy(
            send.at[others], recv.at[others], b_send.at[0], b_recv.at[i], prev, MESH
        )

    fetched(mk_send, mk_recv, 0).wait_recv()

    def weigh(hs, _):
        scores = [dot_nt(q_t[h], mk_recv[slot_of(h)]) * scale for h in hs]
        tops = [jnp.max(x, axis=-1, keepdims=True) for x in scores]
        weights = [jnp.exp(x - t) for x, t in zip(scores, tops)]
        sums = [jnp.sum(w, axis=-1, keepdims=True) for w in weights]
        for h, w, below in zip(hs, weights, sums):
            mem_w[h] = (w * (gate_of(h)[:, :blk] / below)).astype(jnp.bfloat16)
        return 0

    some_heads(UNROLL, weigh)

    lane_all = lax.broadcasted_iota(jnp.int32, (tok, width), 1)
    first_block = group == 0
    for c in range(cn):
        a_direct(c).wait_recv()
    for c in range(pieces):
        s_piece(c).wait_recv()
    by_head(ap_t, ansp_v, 0, tok)

    def join(hs, _):
        stats = stp_v[...]
        tops_p = [jnp.where(lane_all == h, stats, 0.0) for h in hs]
        sums_p = [jnp.where(lane_all == h + heads, stats, 0.0) for h in hs]
        tops_p = [jnp.sum(x, axis=-1, keepdims=True) for x in tops_p]
        sums_p = [jnp.sum(x, axis=-1, keepdims=True) for x in sums_p]
        for h, top_p, sum_p in zip(hs, tops_p, sums_p):
            top_p = jnp.where(first_block, NEG, top_p)
            top_o = own_m[h]
            top = jnp.maximum(top_p, top_o)
            part_p = jnp.exp(top_p - top)
            part_o = jnp.exp(top_o - top)
            mine = own_o[h]
            above = part_p * ap_t[h].astype(jnp.float32) + part_o * mine[:, :width]
            below = part_p * sum_p + part_o * mine[:, width:]
            own_m[h] = (1.0 - gate_of(h)) * (above / below)
        return 0

    some_heads(UNROLL, join)

    fetched(mv_send, mv_recv, 1).wait_recv()

    def recall(hs, _):
        found = [dot_nn(mem_w[h], mv_recv[slot_of(h)]) for h in hs]
        for h, x in zip(hs, found):
            ap_t[h] = (x + own_m[h]).astype(jnp.bfloat16)
        return 0

    some_heads(min(8, heads), recall)

    def result(c):
        rows = pl.ds(c * 16, 16)
        return pltpu.make_async_copy(q_v.at[rows], out_hbm.at[rows], out_sem.at[c])

    for c in range(tok // 16):
        rows = pl.ds(c * 16, 16)
        q_v[rows] = jnp.swapaxes(ap_t[:, rows, :], 0, 1)
        result(c).start()
    ask_all.wait_send()
    for i in range(max(0, 2 * batches - AHEAD), 2 * batches):
        batch_done(i)
    for c in range(cn):
        q_direct(c).wait_send()
        a_direct(c).wait_send()
    for c in range(pieces):
        s_piece(c).wait_send()

    @pl.when(first_ctx)
    def _():
        for j in range(1, cn):
            ask_aside(DOWN + j - 1, j, 0).wait_send()

    @pl.when(last_ctx)
    def _():
        for j in range(cn - 1):
            ask_aside(UP + j, j, 1).wait_send()

    for c in range(tok // 16):
        result(c).wait()


def local(queries, window_keys, window_values, mem_keys, mem_values, gate_logit, block_ids):
    _, tok, heads, width = queries.shape
    held, _, blk, _ = mem_keys.shape
    mem_n, cn = lax.axis_size("mem"), lax.axis_size("ctx")
    zn = mem_n // XN
    pieces = tok // CHUNK
    wanted = block_ids[0, 0]
    anywhere = pl.BlockSpec(memory_space=pl.ANY)
    scalars = pl.BlockSpec(memory_space=pltpu.SMEM)
    bf, f32 = jnp.bfloat16, jnp.float32
    dma = pltpu.SemaphoreType.DMA
    native = pltpu.VMEM((tok, heads, width), bf)
    slots = pltpu.VMEM((mem_n + 2, blk, width), bf)
    out = pl.pallas_call(
        functools.partial(kernel, (XN, zn, cn, held)),
        out_shape=jax.ShapeDtypeStruct((tok, heads, width), bf),
        in_specs=[anywhere] * 5 + [scalars, scalars, anywhere],
        out_specs=anywhere,
        scratch_shapes=[
            native, native, native,
            pltpu.VMEM((held * heads, blk, width), bf),
            pltpu.VMEM((held * heads, blk, width), bf),
            native, native, native,
            pltpu.VMEM((tok, width), f32),
            pltpu.VMEM((tok, width), f32),
            pltpu.VMEM((heads, tok, width), bf),
            pltpu.VMEM((heads, tok, width), bf),
            pltpu.VMEM((heads, tok, 2 * width), bf),
            pltpu.VMEM((heads, CHUNK, width), bf),
            pltpu.VMEM((heads, CHUNK, width), bf),
            pltpu.VMEM((heads, tok, width), bf),
            pltpu.VMEM((heads, tok, 2 * width), f32),
            pltpu.VMEM((heads, tok, width), f32),
            pltpu.VMEM((heads, tok, blk), bf),
            pltpu.VMEM((mem_n + 2, 1, heads), jnp.int32),
            pltpu.VMEM((mem_n + 2, 128), jnp.int32),
            pltpu.SMEM((mem_n + 2, 128), jnp.int32),
            slots, slots, slots, slots,
            dma((5,)), dma((cn,)), dma((cn,)), dma((cn,)), dma((cn,)),
            dma((pieces,)), dma((pieces,)), dma((cn,)), dma((2,)),
            dma, dma, dma((2 * len(PLAN), 4)), dma((2,)), dma, dma, dma((tok // 16,)),
        ],
        compiler_params=pltpu.CompilerParams(
            collective_id=0, has_side_effects=True, vmem_limit_bytes=56 * 1024 * 1024
        ),
    )(
        queries[0], window_keys[0], window_values[0],
        mem_keys.reshape(held * heads, blk, width), mem_values.reshape(held * heads, blk, width),
        gate_logit, wanted, block_ids[0],
    )
    return out[None]


def solution(mesh):
    placed = (
        P("dp", ("mem", "ctx"), None, None),
        P("dp", ("mem", "ctx"), None, None),
        P("dp", ("mem", "ctx"), None, None),
        P("mem", None, None, None),
        P("mem", None, None, None),
        P(),
        P("dp", ("mem", "ctx"), None),
    )
    return jax.shard_map(
        local,
        mesh=mesh,
        in_specs=placed,
        out_specs=P("dp", ("mem", "ctx"), None, None),
        check_vma=False,
    )
```

```python
import functools

import jax
import jax.numpy as jnp
from jax import lax
from jax.experimental import pallas as pl
from jax.experimental.pallas import tpu as pltpu
from jax.sharding import PartitionSpec as P

MESH = pl.DeviceIdType.MESH
XN = 4
CHUNK = 32
UNROLL = 4
NEG = -1e30
AHEAD = 4
DOWN, UP = 17, 28
BOTH, NOT_FIRST, NOT_LAST = range(3)
PLAN = (
    ((20, 4, NOT_FIRST), (28, 4, NOT_LAST)),
    ((17, 3, NOT_FIRST), (32, 3, NOT_LAST), (16, 1, BOTH), (35, 1, BOTH)),
    ((12, 4, BOTH), (36, 4, BOTH)),
    ((8, 4, BOTH), (40, 4, BOTH)),
    ((24, 3, BOTH), (1, 3, BOTH), (27, 1, BOTH)),
    ((4, 4, BOTH), (44, 4, BOTH)),
)
EXTRA = 1


def dot_nt(a, b):
    return lax.dot_general(a, b, (((1,), (1,)), ((), ())), preferred_element_type=jnp.float32)


def dot_nn(a, b):
    return lax.dot_general(a, b, (((1,), (0,)), ((), ())), preferred_element_type=jnp.float32)


def kernel(
    sizes,
    q_hbm, k_hbm, v_hbm, mk_hbm, mv_hbm, gate_sm, ids_sm, ids_hbm,
    out_hbm, near_hbm,
    q_v, k_v, v_v, mk_v, mv_v,
    qn_v, ansn_v, ansp_v, stn_v, stp_v,
    q_t, k_t, v_t, qn_t, an_t, ap_t, own_o, own_m, mem_w,
    tab_v, entry_v, tab_sm, mk_send, mk_recv, mv_send, mv_recv,
    load_sem, q_send, q_recv, a_send, a_recv, s_send, s_recv, far_send, far_recv,
    r_send, r_recv, b_send, b_recv, self_sem, tab_sem, out_sem, near_sem,
):
    xn, zn, cn, held = sizes
    mem_n = xn * zn
    tok, heads, width = q_v.shape
    blk = mk_v.shape[1]
    scale = width ** (-0.5)
    sub = tok // cn
    mem, ctx, dp = lax.axis_index("mem"), lax.axis_index("ctx"), lax.axis_index("dp")
    mx, mz = mem // zn, mem % zn
    group = mem * cn + ctx
    total = mem_n * cn
    before = (group + total - 1) % total
    after = (group + 1) % total
    prev = (before // cn, before % cn, dp)
    nxt = (after // cn, after % cn, dp)
    first_ctx, last_ctx = ctx == 0, ctx == cn - 1
    not_first, not_last = ctx > 0, ctx < cn - 1
    down, up = DOWN + ctx - 1, UP + ctx

    def owner_at(k):
        return ((mx + k % xn) % xn) * zn + (mz + k // xn) % zn

    def asker_at(k):
        return ((mx + xn - k % xn) % xn) * zn + (mz + zn - k // xn) % zn

    loads = [
        pltpu.make_async_copy(src, dst, load_sem.at[i])
        for i, (src, dst) in enumerate(
            ((k_hbm, k_v), (mk_hbm, mk_v), (mv_hbm, mv_v), (v_hbm, v_v), (q_hbm, q_v))
        )
    ]
    for load in loads:
        load.start()
    own_row = pltpu.make_async_copy(ids_hbm, tab_v.at[0], self_sem)
    own_row.start()

    barrier = pltpu.get_barrier_semaphore()

    def greet(k, _):
        pl.semaphore_signal(barrier, inc=1, device_id=(owner_at(k), ctx, dp), device_id_type=MESH)
        return 0

    lax.fori_loop(1, mem_n, greet, 0)

    def greet_at(there):
        pl.semaphore_signal(barrier, inc=1, device_id=there, device_id_type=MESH)

    greet_at(prev)
    greet_at(nxt)

    @pl.when(first_ctx)
    def _():
        for j in range(1, cn):
            greet_at((owner_at(DOWN + j - 1), j, dp))

    @pl.when(last_ctx)
    def _():
        for j in range(cn - 1):
            greet_at((owner_at(UP + j), j, dp))

    pl.when(not_first)(lambda: greet_at((asker_at(down), 0, dp)))
    pl.when(not_last)(lambda: greet_at((asker_at(up), cn - 1, dp)))
    pl.when(first_ctx | last_ctx)(lambda: pl.semaphore_wait(barrier, mem_n + 1 + cn))
    pl.when(not_first & not_last)(lambda: pl.semaphore_wait(barrier, mem_n + 1 + 2))

    def ask(k, _):
        owner = owner_at(k)
        pltpu.make_async_remote_copy(
            ids_hbm, tab_v.at[k], r_send, r_recv, (owner, ctx, dp), MESH
        ).start()
        return 0

    lax.fori_loop(1, mem_n, ask, 0)

    def ask_aside(k, j, i):
        owner = owner_at(k)
        return pltpu.make_async_remote_copy(
            ids_hbm, tab_v.at[mem_n + i], far_send.at[j], far_recv.at[i], (owner, j, dp), MESH
        )

    @pl.when(first_ctx)
    def _():
        for j in range(1, cn):
            ask_aside(DOWN + j - 1, j, 0).start()

    @pl.when(last_ctx)
    def _():
        for j in range(cn - 1):
            ask_aside(UP + j, j, 1).start()

    def rows_of(c):
        return pl.ds(c * sub, sub)

    def q_direct(c):
        return pltpu.make_async_remote_copy(
            q_hbm.at[rows_of(c)], qn_v.at[rows_of(c)], q_send.at[c], q_recv.at[c], prev, MESH
        )

    def q_start(c):
        q_direct(c).start()

    for c in range(min(4, cn)):
        q_start(c)

    def by_head(dst, src, first, count):
        def one(i, _):
            rows = src[pl.ds(first + i * 16, 16)]
            dst[:, pl.ds(i * 16, 16), pl.ds(0, width)] = jnp.swapaxes(rows, 0, 1)
            return 0

        lax.fori_loop(0, count // 16, one, 0)

    def by_position(dst, src, first, count):
        def one(i, _):
            dst[pl.ds(first + i * 16, 16)] = jnp.swapaxes(src[:, pl.ds(i * 16, 16), :], 0, 1)
            return 0

        lax.fori_loop(0, count // 16, one, 0)

    def some_heads(count, body, init=0, first=0, last=heads):
        def one(i, carry):
            return body([i * count + u for u in range(count)], carry)

        return lax.fori_loop(first // count, last // count, one, init)

    loads[0].wait()
    by_head(k_t, k_v, 0, tok)

    others = pl.ds(1, mem_n - 1)
    ask_all = pltpu.make_async_remote_copy(
        tab_v.at[others], tab_v.at[others], r_send, r_recv, prev, MESH
    )
    loads[1].wait()
    own_row.wait()
    ask_all.wait_recv()
    pl.when(not_first)(lambda: ask_aside(0, 0, 0).wait_recv())
    pl.when(not_last)(lambda: ask_aside(0, 0, 1).wait_recv())
    inside = tab_v[:, 0, :] - mem * held
    head_of = lax.broadcasted_iota(jnp.int32, inside.shape, 1)
    entry = jnp.where((inside >= 0) & (inside < held), inside * heads + head_of, 0)
    entry = jnp.sum(entry, axis=-1, keepdims=True)
    entry = jnp.clip(entry, 0, held * heads - 1)
    entry_v[...] = jnp.broadcast_to(entry, entry_v.shape)
    to_scalar = pltpu.make_async_copy(entry_v, tab_sm, tab_sem)
    to_scalar.start()
    to_scalar.wait()

    batches = len(PLAN)
    who = {BOTH: None, NOT_FIRST: not_first, NOT_LAST: not_last}
    extras = {(EXTRA, NOT_FIRST): (mem_n, down, 0), (EXTRA, NOT_LAST): (mem_n + 1, up, cn - 1)}

    def guarded(part, act):
        if who[part] is None:
            act()
        else:
            pl.when(who[part])(act)

    def batch_done(i):
        send = (mk_send, mv_send)[i // batches]
        for r, (first, count, part) in enumerate(PLAN[i % batches]):
            sent = pl.ds(0, count + int((i % batches, part) in extras))
            copy = pltpu.make_async_remote_copy(
                send.at[sent], send.at[sent], b_send.at[i, r], b_recv.at[0], prev, MESH
            )
            guarded(part, copy.wait_send)

    def serve(i):
        send, recv = ((mk_send, mk_recv), (mv_send, mv_recv))[i // batches]
        held_v = (mk_v, mv_v)[i // batches]
        if i >= AHEAD:
            batch_done(i - AHEAD)
        if i % batches == 0:
            recv[0] = held_v[tab_sm[0, 0]]

        def push(k, to, r, there):
            send[k] = held_v[tab_sm[k, 0]]
            pltpu.make_async_remote_copy(
                send.at[k], recv.at[to], b_send.at[i, r], b_recv.at[i // batches], there, MESH
            ).start()

        ranges = PLAN[i % batches]
        for r, (first, count, part) in enumerate(ranges):
            if (i % batches, part) in extras:
                k, to, there = extras[i % batches, part]
                guarded(part, lambda k=k, to=to, r=r, y=there: push(k, to, r, (asker_at(to), y, dp)))

        def some(t, _):
            for r, (first, count, part) in enumerate(ranges):
                if count > 1:
                    k = first + t
                    guarded(part, lambda k=k, r=r: push(k, k, r, (asker_at(k), ctx, dp)))
            return 0

        lax.fori_loop(0, min([count for _, count, _ in ranges if count > 1] or [0]), some, 0)
        for r, (first, count, part) in enumerate(ranges):
            if count == 1:
                guarded(part, lambda k=first, r=r: push(k, k, r, (asker_at(k), ctx, dp)))

    steps = iter(range(2 * batches))

    def pump():
        for i in steps:
            serve(i)
            return

    loads[2].wait()
    pump()
    pump()
    for c in range(4, cn):
        q_start(c)
    pump()

    for i, (src, dst) in ((3, (v_v, v_t)), (4, (q_v, q_t))):
        loads[i].wait()
        by_head(dst, src, 0, tok)
    pump()

    def ones_half(h, _):
        v_t[h, :, pl.ds(width, width)] = jnp.ones((tok, width), jnp.bfloat16)
        return 0

    lax.fori_loop(0, heads, ones_half, 0)

    q_pos = lax.broadcasted_iota(jnp.int32, (tok, tok), 0)
    k_pos = lax.broadcasted_iota(jnp.int32, (tok, tok), 1)

    lane = lax.broadcasted_iota(jnp.int32, (CHUNK, width), 1)

    def a_direct(c):
        return pltpu.make_async_remote_copy(
            ansn_v.at[rows_of(c)], ansp_v.at[rows_of(c)], a_send.at[c], a_recv.at[c], nxt, MESH
        )

    def s_piece(c):
        rows = pl.ds(c * CHUNK, CHUNK)
        return pltpu.make_async_remote_copy(
            stn_v.at[rows], stp_v.at[rows], s_send.at[c], s_recv.at[c], nxt, MESH
        )

    per = CHUNK // sub

    def answer(c):
        for j in range(c * per, (c + 1) * per):
            q_direct(j).wait_recv()
        by_head(qn_t, qn_v, c * CHUNK, CHUNK)
        past = k_pos[:CHUNK] > q_pos[:CHUNK] + c * CHUNK

        def partial(hs, stats):
            scores = [dot_nt(qn_t[h], k_t[h]) for h in hs]
            scores = [jnp.where(past, x * scale, NEG) for x in scores]
            tops = [jnp.max(x, axis=-1, keepdims=True) for x in scores]
            weights = [jnp.where(past, jnp.exp(x - t), 0.0) for x, t in zip(scores, tops)]
            summed = [dot_nn(w.astype(jnp.bfloat16), v_t[h]) for w, h in zip(weights, hs)]
            for h, x, t in zip(hs, summed, tops):
                an_t[h] = x[:, :width].astype(jnp.bfloat16)
                stats = jnp.where(lane == h, t, stats)
                stats = jnp.where(lane == h + heads, x[:, width:], stats)
            return stats

        stn_v[pl.ds(c * CHUNK, CHUNK)] = some_heads(
            min(8, heads), partial, jnp.zeros((CHUNK, width), jnp.float32)
        )
        by_position(ansn_v, an_t, c * CHUNK, CHUNK)
        for j in range(c * per, (c + 1) * per):
            a_direct(j).start()
        s_piece(c).start()

    causal = k_pos <= q_pos

    def own(hs, _):
        scores = [dot_nt(q_t[h], k_t[h]) for h in hs]
        scores = [jnp.where(causal, x * scale, NEG) for x in scores]
        tops = [jnp.max(x, axis=-1, keepdims=True) for x in scores]
        weights = [jnp.exp(x - t).astype(jnp.bfloat16) for x, t in zip(scores, tops)]
        summed = [dot_nn(w, v_t[h]) for w, h in zip(weights, hs)]
        for h, x, t in zip(hs, summed, tops):
            own_o[h] = x
            own_m[h] = jnp.broadcast_to(t, (tok, width))
        return 0

    pieces = tok // CHUNK
    for c in range(pieces // 2):
        answer(c)
        pump()
    some_heads(UNROLL, own)
    pump()
    for c in range(pieces // 2, pieces):
        answer(c)
        pump()
    for _ in range(2 * batches):
        pump()

    def gate_of(h):
        return 1.0 / (1.0 + jnp.exp(jnp.full((8, width), -gate_sm[h], jnp.float32)))[:1]

    def slot_of(h):
        owner = lax.div(ids_sm[h], held)
        dx = lax.rem(lax.div(owner, zn) - mx + xn, xn)
        dz = lax.rem(lax.rem(owner, zn) - mz + zn, zn)
        return dz * xn + dx

    def fetched(send, recv, i):
        return pltpu.make_async_remote_copy(
            send.at[others], recv.at[others], b_send.at[0], b_recv.at[i], prev, MESH
        )

    fetched(mk_send, mk_recv, 0).wait_recv()

    def weigh(hs, _):
        scores = [dot_nt(q_t[h], mk_recv[slot_of(h)]) * scale for h in hs]
        tops = [jnp.max(x, axis=-1, keepdims=True) for x in scores]
        weights = [jnp.exp(x - t) for x, t in zip(scores, tops)]
        sums = [jnp.sum(w, axis=-1, keepdims=True) for w in weights]
        for h, w, below in zip(hs, weights, sums):
            mem_w[h] = (w * (gate_of(h)[:, :blk] / below)).astype(jnp.bfloat16)
        return 0

    some_heads(UNROLL, weigh)

    lane_all = lax.broadcasted_iota(jnp.int32, (tok, width), 1)
    first_block = group == 0
    for c in range(cn):
        a_direct(c).wait_recv()
    for c in range(pieces):
        s_piece(c).wait_recv()
    by_head(ap_t, ansp_v, 0, tok)

    def join(hs, _):
        stats = stp_v[...]
        tops_p = [jnp.where(lane_all == h, stats, 0.0) for h in hs]
        sums_p = [jnp.where(lane_all == h + heads, stats, 0.0) for h in hs]
        tops_p = [jnp.sum(x, axis=-1, keepdims=True) for x in tops_p]
        sums_p = [jnp.sum(x, axis=-1, keepdims=True) for x in sums_p]
        for h, top_p, sum_p in zip(hs, tops_p, sums_p):
            top_p = jnp.where(first_block, NEG, top_p)
            top_o = own_m[h]
            top = jnp.maximum(top_p, top_o)
            part_p = jnp.exp(top_p - top)
            part_o = jnp.exp(top_o - top)
            mine = own_o[h]
            above = part_p * ap_t[h].astype(jnp.float32) + part_o * mine[:, :width]
            below = part_p * sum_p + part_o * mine[:, width:]
            ap_t[h] = ((1.0 - gate_of(h)) * (above / below)).astype(jnp.bfloat16)
        return 0

    some_heads(UNROLL, join)

    def near(c):
        rows = pl.ds(c * 16, 16)
        return pltpu.make_async_copy(k_v.at[rows], near_hbm.at[rows], near_sem.at[c])

    for c in range(tok // 16):
        rows = pl.ds(c * 16, 16)
        k_v[rows] = jnp.swapaxes(ap_t[:, rows, :], 0, 1)
        near(c).start()

    fetched(mv_send, mv_recv, 1).wait_recv()

    def recall(hs, _):
        found = [dot_nn(mem_w[h], mv_recv[slot_of(h)]) for h in hs]
        for h, x in zip(hs, found):
            ap_t[h] = x.astype(jnp.bfloat16)
        return 0

    some_heads(min(8, heads), recall)

    def result(c):
        rows = pl.ds(c * 16, 16)
        return pltpu.make_async_copy(q_v.at[rows], out_hbm.at[rows], out_sem.at[c])

    for c in range(tok // 16):
        rows = pl.ds(c * 16, 16)
        q_v[rows] = jnp.swapaxes(ap_t[:, rows, :], 0, 1)
        result(c).start()
    ask_all.wait_send()
    for i in range(max(0, 2 * batches - AHEAD), 2 * batches):
        batch_done(i)
    for c in range(cn):
        q_direct(c).wait_send()
        a_direct(c).wait_send()
    for c in range(pieces):
        s_piece(c).wait_send()

    @pl.when(first_ctx)
    def _():
        for j in range(1, cn):
            ask_aside(DOWN + j - 1, j, 0).wait_send()

    @pl.when(last_ctx)
    def _():
        for j in range(cn - 1):
            ask_aside(UP + j, j, 1).wait_send()

    for c in range(tok // 16):
        near(c).wait()
        result(c).wait()


def local(queries, window_keys, window_values, mem_keys, mem_values, gate_logit, block_ids):
    _, tok, heads, width = queries.shape
    held, _, blk, _ = mem_keys.shape
    mem_n, cn = lax.axis_size("mem"), lax.axis_size("ctx")
    zn = mem_n // XN
    pieces = tok // CHUNK
    wanted = block_ids[0, 0]
    anywhere = pl.BlockSpec(memory_space=pl.ANY)
    scalars = pl.BlockSpec(memory_space=pltpu.SMEM)
    bf, f32 = jnp.bfloat16, jnp.float32
    dma = pltpu.SemaphoreType.DMA
    native = pltpu.VMEM((tok, heads, width), bf)
    slots = pltpu.VMEM((mem_n + 2, blk, width), bf)
    far_part, near_part = pl.pallas_call(
        functools.partial(kernel, (XN, zn, cn, held)),
        out_shape=[jax.ShapeDtypeStruct((tok, heads, width), bf)] * 2,
        in_specs=[anywhere] * 5 + [scalars, scalars, anywhere],
        out_specs=[anywhere] * 2,
        scratch_shapes=[
            native, native, native,
            pltpu.VMEM((held * heads, blk, width), bf),
            pltpu.VMEM((held * heads, blk, width), bf),
            native, native, native,
            pltpu.VMEM((tok, width), f32),
            pltpu.VMEM((tok, width), f32),
            pltpu.VMEM((heads, tok, width), bf),
            pltpu.VMEM((heads, tok, width), bf),
            pltpu.VMEM((heads, tok, 2 * width), bf),
            pltpu.VMEM((heads, CHUNK, width), bf),
            pltpu.VMEM((heads, CHUNK, width), bf),
            pltpu.VMEM((heads, tok, width), bf),
            pltpu.VMEM((heads, tok, 2 * width), f32),
            pltpu.VMEM((heads, tok, width), f32),
            pltpu.VMEM((heads, tok, blk), bf),
            pltpu.VMEM((mem_n + 2, 1, heads), jnp.int32),
            pltpu.VMEM((mem_n + 2, 128), jnp.int32),
            pltpu.SMEM((mem_n + 2, 128), jnp.int32),
            slots, slots, slots, slots,
            dma((5,)), dma((cn,)), dma((cn,)), dma((cn,)), dma((cn,)),
            dma((pieces,)), dma((pieces,)), dma((cn,)), dma((2,)),
            dma, dma, dma((2 * len(PLAN), 4)), dma((2,)), dma, dma, dma((tok // 16,)), dma((tok // 16,)),
        ],
        compiler_params=pltpu.CompilerParams(
            collective_id=0, has_side_effects=True, vmem_limit_bytes=56 * 1024 * 1024
        ),
    )(
        queries[0], window_keys[0], window_values[0],
        mem_keys.reshape(held * heads, blk, width), mem_values.reshape(held * heads, blk, width),
        gate_logit, wanted, block_ids[0],
    )
    return (far_part.astype(f32) + near_part.astype(f32)).astype(bf)[None]


def solution(mesh):
    placed = (
        P("dp", ("mem", "ctx"), None, None),
        P("dp", ("mem", "ctx"), None, None),
        P("dp", ("mem", "ctx"), None, None),
        P("mem", None, None, None),
        P("mem", None, None, None),
        P(),
        P("dp", ("mem", "ctx"), None),
    )
    return jax.shard_map(
        local,
        mesh=mesh,
        in_specs=placed,
        out_specs=P("dp", ("mem", "ctx"), None, None),
        check_vma=False,
    )
```
